32 devices in a mesh: blk: 8 (over z, y), ulysses: 4 (over x, core).
Axes of the slice: x: 2, y: 2, z: 4, core: 2. Of those that a mesh axis runs over, the one named last changes fastest.
Arguments:
- queries: bfloat16 [192, 4096], P(('blk', 'ulysses')), may hold values from -8 to 8
- key_vectors: bfloat16 [192, 4096], P(('blk', 'ulysses')), may hold values from -8 to 8
- value_vectors: bfloat16 [192, 4096], P(('blk', 'ulysses')), may hold values from -12 to 12
- cotangent: bfloat16 [192, 4096], P(('blk', 'ulysses')), may hold values from -192 to 192
Outputs:
- grad_queries: bfloat16 [192, 4096], P(('blk', 'ulysses'))
- grad_keys: bfloat16 [192, 4096], P(('blk', 'ulysses'))
- grad_values: bfloat16 [192, 4096], P(('blk', 'ulysses'))
The draws below stay inside these ranges and needn't reach their ends.
All inputs are finite; a program needn't handle non-finite values.
Results may differ from the reference program's by a relative error of at most 0.0067.
Values may be sent and summed in bfloat16 or wider, within the bound.
No kernel may reach another device: no remote copies, remote signals or barrier semaphores. Data moves between devices by JAX's collectives and lax.ppermute only.
A program may use at most 64 MiB of HBM per device.

```python
import math
import jax
import jax.numpy as jnp
from jax import lax

HEADS = 32
D_HEAD = 128
TOKENS = 192


def drawn_draw(key, which_arg):
    columns = HEADS * D_HEAD
    noise_key = jax.random.fold_in(key, 101 + which_arg)
    result_array = jnp.clip(jax.random.normal(noise_key, (TOKENS, columns), jnp.float32), -5.0, 5.0)
    return result_array.astype(jnp.bfloat16)


def draw_queries(key, part):
    return drawn_draw(key, 0)


def draw_key_vectors(key, part):
    return drawn_draw(key, 1)


def shard_levels(rng, dims, cuts, smallest, high):
    def one(dim, parts):
        draws = jax.random.uniform(jax.random.fold_in(jax.random.fold_in(rng, 6), dim), (parts,), jnp.float32, smallest / len(cuts), high / len(cuts))
        return jnp.repeat(jnp.exp(draws), dims[dim] // parts).reshape((-1,) + (1,) * (len(dims) - dim - 1))

    gain = one(*cuts[0])
    for cut in cuts[1:]:
        gain = gain * one(*cut)
    return gain


def scatter_about(own_key, dims, deviation, most, split=(), held_as=jnp.bfloat16):
    array = jax.random.normal(own_key, dims, jnp.float32) * deviation
    if len(split) > 0:
        array = shard_levels(own_key, dims, split, -0.22, 0.18) * array
    return jnp.clip(array, min=-most, max=most).astype(held_as)


def setup_inputs(seed: int = 0) -> dict:
    streams_of = jax.random.split(jax.random.key(seed), 5)
    return {
        "queries": draw_queries(jax.random.fold_in(streams_of[4], 71), 0),
        "key_vectors": draw_key_vectors(jax.random.fold_in(streams_of[4], 71), 0),
        "value_vectors": scatter_about(streams_of[2], (TOKENS, HEADS * D_HEAD), 2.0, 12.0, ((0, 32),)),
        "cotangent": scatter_about(streams_of[3], (TOKENS, HEADS * D_HEAD), 32.0, 192.0, ((0, 32),)),
    }


def one_head(operands):
    query_head, key_head, value_head, grad_head = operands
    score_scale = 1.0 / math.sqrt(D_HEAD)
    logits = jnp.dot(query_head, key_head.T, preferred_element_type=jnp.float32) * score_scale
    row_top = lax.optimization_barrier(jnp.max(logits, axis=1, keepdims=True))
    log_total = row_top + jnp.log(lax.optimization_barrier(jnp.sum(jnp.exp(logits - row_top), axis=1, keepdims=True)))
    weights = jnp.exp(logits - log_total)
    grad_weights = jnp.dot(grad_head, value_head.T, preferred_element_type=jnp.float32)
    row_dot = lax.optimization_barrier(jnp.sum(weights * grad_weights, axis=1, keepdims=True))
    grad_logits = weights * (grad_weights - row_dot)
    weights_low = weights.astype(jnp.bfloat16)
    grad_low = grad_logits.astype(jnp.bfloat16)
    grad_query = (jnp.dot(grad_low, key_head, preferred_element_type=jnp.float32) * score_scale).astype(jnp.bfloat16)
    grad_key = (jnp.dot(grad_low.T, query_head, preferred_element_type=jnp.float32) * score_scale).astype(jnp.bfloat16)
    grad_value = jnp.dot(weights_low.T, grad_head, preferred_element_type=jnp.float32).astype(jnp.bfloat16)
    return (grad_query, grad_key, grad_value)

def reference(queries, key_vectors, value_vectors, cotangent):

    def heads_first(matrix):
        return matrix.reshape(TOKENS, HEADS, D_HEAD).transpose(1, 0, 2)

    def rows_first(stacked):
        return stacked.transpose(1, 0, 2).reshape(TOKENS, HEADS * D_HEAD)
    grads = lax.map(one_head, (heads_first(queries), heads_first(key_vectors), heads_first(value_vectors), heads_first(cotangent)))
    return (rows_first(grads[0]), rows_first(grads[1]), rows_first(grads[2]))
```

```python
import math

import jax
import jax.numpy as jnp
from jax import lax
from jax.experimental import pallas as pl
from jax.experimental.pallas import tpu as pltpu
from jax.sharding import PartitionSpec as P

HEADS = 32
D_HEAD = 128
AXES = ("blk", "ulysses")
VMEM = pl.BlockSpec(memory_space=pltpu.VMEM)


def pack_kernel(query_ref, key_ref, value_ref, grad_ref, out_ref):
    rows = query_ref.shape[0]
    heads = out_ref.shape[0]
    for head in range(heads):
        columns = slice(head * D_HEAD, (head + 1) * D_HEAD)
        parts = [
            ref[:, columns].astype(jnp.float32)
            for ref in (query_ref, key_ref, value_ref, grad_ref)
        ]
        out_ref[head] = jnp.concatenate(parts, axis=0).astype(jnp.bfloat16)


def dot(left, right, left_dim, right_dim):
    return lax.dot_general(
        left, right, (((left_dim,), (right_dim,)), ((), ())), preferred_element_type=jnp.float32
    )


def head_kernel(rows, in_ref, out_ref):
    senders = in_ref.shape[0]
    score_scale = 1.0 / math.sqrt(D_HEAD)
    blocks = [in_ref[sender].astype(jnp.float32) for sender in range(senders)]

    def gathered(which):
        return jnp.concatenate(
            [block[which * rows : (which + 1) * rows] for block in blocks], axis=0
        ).astype(jnp.bfloat16)

    query, key, value, grad = (gathered(which) for which in range(4))
    logits = dot(query, key, 1, 1) * score_scale
    top = jnp.max(logits, axis=1, keepdims=True)
    terms = jnp.exp(logits - top)
    weights = terms / jnp.sum(terms, axis=1, keepdims=True)
    grad_weights = dot(grad, value, 1, 1)
    row_dot = jnp.sum(weights * grad_weights, axis=1, keepdims=True)
    grad_low = (weights * (grad_weights - row_dot)).astype(jnp.bfloat16)
    weights_low = weights.astype(jnp.bfloat16)
    grad_query = dot(grad_low, key, 1, 0) * score_scale
    grad_key = dot(grad_low, query, 0, 0) * score_scale
    grad_value = dot(weights_low, grad, 0, 0)
    for sender in range(senders):
        own = slice(sender * rows, (sender + 1) * rows)
        out_ref[sender, : 3 * rows] = jnp.concatenate(
            [grad_query[own], grad_key[own], grad_value[own]], axis=0
        ).astype(jnp.bfloat16)
    out_ref[:, 3 * rows :] = jnp.zeros_like(out_ref[:, 3 * rows :])


def unpack_kernel(in_ref, query_ref, key_ref, value_ref):
    rows = query_ref.shape[0]
    for head in range(in_ref.shape[0]):
        block = in_ref[head].astype(jnp.float32)
        columns = slice(head * D_HEAD, (head + 1) * D_HEAD)
        for which, ref in enumerate((query_ref, key_ref, value_ref)):
            ref[:, columns] = block[which * rows : (which + 1) * rows].astype(jnp.bfloat16)


def by_head(queries, key_vectors, value_vectors, cotangent):
    rows = queries.shape[0]
    sent = jax.ShapeDtypeStruct((HEADS, 4 * rows, D_HEAD), jnp.bfloat16)
    packed = pl.pallas_call(
        pack_kernel, out_shape=sent, in_specs=[VMEM] * 4, out_specs=VMEM
    )(queries, key_vectors, value_vectors, cotangent)
    held = lax.all_to_all(packed, AXES, split_axis=0, concat_axis=0, tiled=True)
    back = pl.pallas_call(
        lambda *refs: head_kernel(rows, *refs), out_shape=sent, in_specs=[VMEM], out_specs=VMEM
    )(held)
    back = lax.all_to_all(back, AXES, split_axis=0, concat_axis=0, tiled=True)
    out = jax.ShapeDtypeStruct(queries.shape, jnp.bfloat16)
    return pl.pallas_call(
        unpack_kernel, out_shape=(out,) * 3, in_specs=[VMEM], out_specs=(VMEM,) * 3
    )(back)


def scores(query_part, key_part, score_scale):
    return (
        jnp.einsum("qhd,khd->hqk", query_part, key_part, preferred_element_type=jnp.float32)
        * score_scale
    )


def by_block(queries, key_vectors, value_vectors, cotangent):
    ulysses_size = lax.axis_size("ulysses")
    head_dev = HEADS // ulysses_size
    score_scale = 1.0 / math.sqrt(D_HEAD)
    query_heads, key_heads, value_heads, grad_heads = (
        lax.all_to_all(queries, "ulysses", split_axis=1, concat_axis=0, tiled=True),
        lax.all_to_all(key_vectors, "ulysses", split_axis=1, concat_axis=0, tiled=True),
        lax.all_to_all(value_vectors, "ulysses", split_axis=1, concat_axis=0, tiled=True),
        lax.all_to_all(cotangent, "ulysses", split_axis=1, concat_axis=0, tiled=True),
    )
    local_rows = query_heads.shape[0]

    def split_heads(matrix):
        return matrix.reshape(matrix.shape[0], head_dev, D_HEAD)

    own_query = split_heads(query_heads)
    own_key = split_heads(key_heads)
    own_value = split_heads(value_heads)
    own_grad = split_heads(grad_heads)
    held_key, held_value = (
        lax.all_gather(key_heads, "blk", axis=0, tiled=True),
        lax.all_gather(value_heads, "blk", axis=0, tiled=True),
    )
    held_key = split_heads(held_key)
    held_value = split_heads(held_value)
    logits = scores(own_query, held_key, score_scale)
    grad_weights = jnp.einsum(
        "qhd,khd->hqk", own_grad, held_value, preferred_element_type=jnp.float32
    )
    block_top = jnp.max(logits, axis=2)
    exp_terms = jnp.exp(logits - block_top[:, :, None])
    row_total = jnp.sum(exp_terms, axis=2)
    row_sum = jnp.sum(exp_terms * grad_weights, axis=2)
    log_total = block_top + jnp.log(row_total)
    row_dot = row_sum / row_total
    all_log, all_dot = (
        lax.all_gather(log_total.T, "blk", axis=0, tiled=True),
        lax.all_gather(row_dot.T, "blk", axis=0, tiled=True),
    )
    logits = scores(own_query, held_key, score_scale)
    weights = jnp.exp(logits - log_total[:, :, None])
    grad_weights = jnp.einsum(
        "qhd,khd->hqk", own_grad, held_value, preferred_element_type=jnp.float32
    )
    grad_low = (weights * (grad_weights - row_dot[:, :, None])).astype(jnp.bfloat16)
    grad_query = jnp.einsum("hqk,khd->qhd", grad_low, held_key, preferred_element_type=jnp.float32)
    remote_query = split_heads(lax.all_gather(query_heads, "blk", axis=0, tiled=True))
    remote_grad = split_heads(lax.all_gather(grad_heads, "blk", axis=0, tiled=True))
    logits = scores(remote_query, own_key, score_scale)
    weights = jnp.exp(logits - all_log.T[:, :, None])
    grad_weights = jnp.einsum(
        "qhd,khd->hqk", remote_grad, own_value, preferred_element_type=jnp.float32
    )
    grad_low = (weights * (grad_weights - all_dot.T[:, :, None])).astype(jnp.bfloat16)
    weights_low = weights.astype(jnp.bfloat16)
    grad_key = jnp.einsum(
        "hqk,qhd->khd", grad_low, remote_query, preferred_element_type=jnp.float32
    )
    grad_value = jnp.einsum(
        "hqk,qhd->khd", weights_low, remote_grad, preferred_element_type=jnp.float32
    )
    grad_key, grad_value = (grad_key, grad_value)

    def to_rows(summed, factor):
        return (summed * factor).astype(jnp.bfloat16).reshape(local_rows, head_dev * D_HEAD)

    return (
        lax.all_to_all(
            to_rows(grad_query, score_scale), "ulysses", split_axis=0, concat_axis=1, tiled=True
        ),
        lax.all_to_all(
            to_rows(grad_key, score_scale), "ulysses", split_axis=0, concat_axis=1, tiled=True
        ),
        lax.all_to_all(
            to_rows(grad_value, 1.0), "ulysses", split_axis=0, concat_axis=1, tiled=True
        ),
    )


def solution(mesh):
    placed = (
        P(("blk", "ulysses"), None),
        P(("blk", "ulysses"), None),
        P(("blk", "ulysses"), None),
        P(("blk", "ulysses"), None),
    )
    local = by_head if mesh.size == HEADS else by_block
    return jax.shard_map(
        local,
        mesh=mesh,
        in_specs=placed,
        out_specs=(
            P(("blk", "ulysses"), None),
            P(("blk", "ulysses"), None),
            P(("blk", "ulysses"), None),
        ),
        check_vma=False,
    )
```

```python
import math

import jax
import jax.numpy as jnp
from jax import lax
from jax.experimental import pallas as pl
from jax.experimental.pallas import tpu as pltpu
from jax.sharding import PartitionSpec as P

HEADS = 32
D_HEAD = 128
AXES = ("blk", "ulysses")
HBM = pl.BlockSpec(memory_space=pltpu.HBM)
VMEM = pl.BlockSpec(memory_space=pltpu.VMEM)
PARAMS = pltpu.CompilerParams(vmem_limit_bytes=8 * 2**20)


def pack_kernel(query_ref, key_ref, value_ref, grad_ref, out_ref, held, arrived):
    copies = [
        pltpu.make_async_copy(ref, held.at[which], arrived.at[which])
        for which, ref in enumerate((query_ref, key_ref, value_ref, grad_ref))
    ]
    for copy in copies:
        copy.start()
    for copy in copies:
        copy.wait()
    for head in range(out_ref.shape[0]):
        columns = slice(head * D_HEAD, (head + 1) * D_HEAD)
        parts = [held[which, :, columns].astype(jnp.float32) for which in range(4)]
        out_ref[head] = jnp.concatenate(parts, axis=0).astype(jnp.bfloat16)


def dot(left, right, left_dim, right_dim):
    return lax.dot_general(
        left, right, (((left_dim,), (right_dim,)), ((), ())), preferred_element_type=jnp.float32
    )


def head_kernel(rows, in_ref, out_ref):
    senders = in_ref.shape[0]
    score_scale = 1.0 / math.sqrt(D_HEAD)
    blocks = [in_ref[sender].astype(jnp.float32) for sender in range(senders)]

    def gathered(which):
        return jnp.concatenate(
            [block[which * rows : (which + 1) * rows] for block in blocks], axis=0
        ).astype(jnp.bfloat16)

    query, key, value, grad = (gathered(which) for which in range(4))
    logits = dot(query, key, 1, 1) * score_scale
    top = jnp.max(logits, axis=1, keepdims=True)
    terms = jnp.exp(logits - top)
    weights = terms / jnp.sum(terms, axis=1, keepdims=True)
    grad_weights = dot(grad, value, 1, 1)
    row_dot = jnp.sum(weights * grad_weights, axis=1, keepdims=True)
    grad_low = (weights * (grad_weights - row_dot)).astype(jnp.bfloat16)
    weights_low = weights.astype(jnp.bfloat16)
    grads = (
        dot(grad_low, key, 1, 0) * score_scale,
        dot(grad_low, query, 0, 0) * score_scale,
        dot(weights_low, grad, 0, 0),
    )
    out_ref[...] = jnp.concatenate(
        [
            total[sender * rows : (sender + 1) * rows]
            for sender in range(senders)
            for total in grads
        ],
        axis=0,
    ).astype(jnp.bfloat16)


def unpack_kernel(in_ref, query_ref, key_ref, value_ref):
    rows = query_ref.shape[0]
    heads = in_ref.shape[0] // (3 * rows)
    received = in_ref[...].astype(jnp.float32)
    for which, ref in enumerate((query_ref, key_ref, value_ref)):
        for head in range(heads):
            first = (3 * head + which) * rows
            columns = slice(head * D_HEAD, (head + 1) * D_HEAD)
            ref[:, columns] = received[first : first + rows].astype(jnp.bfloat16)


def by_head(queries, key_vectors, value_vectors, cotangent):
    rows = queries.shape[0]
    packed = pl.pallas_call(
        pack_kernel,
        out_shape=jax.ShapeDtypeStruct((HEADS, 4 * rows, D_HEAD), jnp.bfloat16),
        in_specs=[HBM] * 4,
        out_specs=VMEM,
        scratch_shapes=[
            pltpu.VMEM((4,) + queries.shape, jnp.bfloat16),
            pltpu.SemaphoreType.DMA((4,)),
        ],
        compiler_params=PARAMS,
    )(*(
        pltpu.with_memory_space_constraint(array, pltpu.HBM)
        for array in (queries, key_vectors, value_vectors, cotangent)
    ))
    held = lax.all_to_all(packed, AXES, split_axis=0, concat_axis=0, tiled=True)
    grads = jax.ShapeDtypeStruct((HEADS * 3 * rows, D_HEAD), jnp.bfloat16)
    back = pl.pallas_call(
        lambda *refs: head_kernel(rows, *refs),
        out_shape=grads,
        in_specs=[VMEM],
        out_specs=VMEM,
        compiler_params=PARAMS,
    )(held)
    pair = math.gcd(rows, 2)
    back = lax.all_to_all(
        back.reshape(HEADS, 3 * rows // pair, pair, D_HEAD),
        AXES,
        split_axis=0,
        concat_axis=0,
        tiled=True,
    )
    out = jax.ShapeDtypeStruct(queries.shape, jnp.bfloat16)
    return pl.pallas_call(
        unpack_kernel,
        out_shape=(out,) * 3,
        in_specs=[VMEM],
        out_specs=(VMEM,) * 3,
        compiler_params=PARAMS,
    )(back.reshape(grads.shape))


def scores(query_part, key_part, score_scale):
    return (
        jnp.einsum("qhd,khd->hqk", query_part, key_part, preferred_element_type=jnp.float32)
        * score_scale
    )


def by_block(queries, key_vectors, value_vectors, cotangent):
    ulysses_size = lax.axis_size("ulysses")
    head_dev = HEADS // ulysses_size
    score_scale = 1.0 / math.sqrt(D_HEAD)
    query_heads, key_heads, value_heads, grad_heads = (
        lax.all_to_all(queries, "ulysses", split_axis=1, concat_axis=0, tiled=True),
        lax.all_to_all(key_vectors, "ulysses", split_axis=1, concat_axis=0, tiled=True),
        lax.all_to_all(value_vectors, "ulysses", split_axis=1, concat_axis=0, tiled=True),
        lax.all_to_all(cotangent, "ulysses", split_axis=1, concat_axis=0, tiled=True),
    )
    local_rows = query_heads.shape[0]

    def split_heads(matrix):
        return matrix.reshape(matrix.shape[0], head_dev, D_HEAD)

    own_query = split_heads(query_heads)
    own_key = split_heads(key_heads)
    own_value = split_heads(value_heads)
    own_grad = split_heads(grad_heads)
    held_key, held_value = (
        lax.all_gather(key_heads, "blk", axis=0, tiled=True),
        lax.all_gather(value_heads, "blk", axis=0, tiled=True),
    )
    held_key = split_heads(held_key)
    held_value = split_heads(held_value)
    logits = scores(own_query, held_key, score_scale)
    grad_weights = jnp.einsum(
        "qhd,khd->hqk", own_grad, held_value, preferred_element_type=jnp.float32
    )
    block_top = jnp.max(logits, axis=2)
    exp_terms = jnp.exp(logits - block_top[:, :, None])
    row_total = jnp.sum(exp_terms, axis=2)
    row_sum = jnp.sum(exp_terms * grad_weights, axis=2)
    log_total = block_top + jnp.log(row_total)
    row_dot = row_sum / row_total
    all_log, all_dot = (
        lax.all_gather(log_total.T, "blk", axis=0, tiled=True),
        lax.all_gather(row_dot.T, "blk", axis=0, tiled=True),
    )
    logits = scores(own_query, held_key, score_scale)
    weights = jnp.exp(logits - log_total[:, :, None])
    grad_weights = jnp.einsum(
        "qhd,khd->hqk", own_grad, held_value, preferred_element_type=jnp.float32
    )
    grad_low = (weights * (grad_weights - row_dot[:, :, None])).astype(jnp.bfloat16)
    grad_query = jnp.einsum("hqk,khd->qhd", grad_low, held_key, preferred_element_type=jnp.float32)
    remote_query = split_heads(lax.all_gather(query_heads, "blk", axis=0, tiled=True))
    remote_grad = split_heads(lax.all_gather(grad_heads, "blk", axis=0, tiled=True))
    logits = scores(remote_query, own_key, score_scale)
    weights = jnp.exp(logits - all_log.T[:, :, None])
    grad_weights = jnp.einsum(
        "qhd,khd->hqk", remote_grad, own_value, preferred_element_type=jnp.float32
    )
    grad_low = (weights * (grad_weights - all_dot.T[:, :, None])).astype(jnp.bfloat16)
    weights_low = weights.astype(jnp.bfloat16)
    grad_key = jnp.einsum(
        "hqk,qhd->khd", grad_low, remote_query, preferred_element_type=jnp.float32
    )
    grad_value = jnp.einsum(
        "hqk,qhd->khd", weights_low, remote_grad, preferred_element_type=jnp.float32
    )
    grad_key, grad_value = (grad_key, grad_value)

    def to_rows(summed, factor):
        return (summed * factor).astype(jnp.bfloat16).reshape(local_rows, head_dev * D_HEAD)

    return (
        lax.all_to_all(
            to_rows(grad_query, score_scale), "ulysses", split_axis=0, concat_axis=1, tiled=True
        ),
        lax.all_to_all(
            to_rows(grad_key, score_scale), "ulysses", split_axis=0, concat_axis=1, tiled=True
        ),
        lax.all_to_all(
            to_rows(grad_value, 1.0), "ulysses", split_axis=0, concat_axis=1, tiled=True
        ),
    )


def solution(mesh):
    placed = (
        P(("blk", "ulysses"), None),
        P(("blk", "ulysses"), None),
        P(("blk", "ulysses"), None),
        P(("blk", "ulysses"), None),
    )
    local = by_head if mesh.size == HEADS else by_block
    return jax.shard_map(
        local,
        mesh=mesh,
        in_specs=placed,
        out_specs=(
            P(("blk", "ulysses"), None),
            P(("blk", "ulysses"), None),
            P(("blk", "ulysses"), None),
        ),
        check_vma=False,
    )
```

```python
import math

import jax
import jax.numpy as jnp
import numpy as np
from jax import lax
from jax.experimental import pallas as pl
from jax.experimental.pallas import tpu as pltpu
from jax.sharding import PartitionSpec as P

HEADS = 32
D_HEAD = 128
AXES = ("blk", "ulysses")
HBM = pl.BlockSpec(memory_space=pltpu.HBM)
VMEM = pl.BlockSpec(memory_space=pltpu.VMEM)
PARAMS = pltpu.CompilerParams(vmem_limit_bytes=8 * 2**20)


def pack_kernel(query_ref, key_ref, value_ref, grad_ref, out_ref, held, arrived):
    copies = [
        pltpu.make_async_copy(ref, held.at[which], arrived.at[which])
        for which, ref in enumerate((query_ref, key_ref, value_ref, grad_ref))
    ]
    for copy in copies:
        copy.start()
    for copy in copies:
        copy.wait()
    for head in range(out_ref.shape[0]):
        columns = slice(head * D_HEAD, (head + 1) * D_HEAD)
        parts = [held[which, :, columns].astype(jnp.float32) for which in range(4)]
        out_ref[head] = jnp.concatenate(parts, axis=0).astype(jnp.bfloat16)


def dot(left, right, left_dim, right_dim):
    return lax.dot_general(
        left, right, (((left_dim,), (right_dim,)), ((), ())), preferred_element_type=jnp.float32
    )


def head_kernel(rows, in_ref, out_ref):
    senders = in_ref.shape[0]
    score_scale = 1.0 / math.sqrt(D_HEAD)
    blocks = [in_ref[sender].astype(jnp.float32) for sender in range(senders)]

    def gathered(which):
        return jnp.concatenate(
            [block[which * rows : (which + 1) * rows] for block in blocks], axis=0
        ).astype(jnp.bfloat16)

    query, key, value, grad = (gathered(which) for which in range(4))
    logits = dot(query, key, 1, 1) * score_scale
    top = jnp.max(logits, axis=1, keepdims=True)
    terms = jnp.exp(logits - top)
    weights = terms / jnp.sum(terms, axis=1, keepdims=True)
    grad_weights = dot(grad, value, 1, 1)
    row_dot = jnp.sum(weights * grad_weights, axis=1, keepdims=True)
    grad_low = (weights * (grad_weights - row_dot)).astype(jnp.bfloat16)
    weights_low = weights.astype(jnp.bfloat16)
    grads = (
        dot(grad_low, key, 1, 0) * score_scale,
        dot(grad_low, query, 0, 0) * score_scale,
        dot(weights_low, grad, 0, 0),
    )
    out_ref[...] = jnp.concatenate(
        [
            total[sender * rows : (sender + 1) * rows]
            for sender in range(senders)
            for total in grads
        ],
        axis=0,
    ).astype(jnp.bfloat16)


def unpack_kernel(in_ref, query_ref, key_ref, value_ref):
    rows = query_ref.shape[0]
    heads = in_ref.shape[0] // (3 * rows)
    received = in_ref[...].astype(jnp.float32)
    for which, ref in enumerate((query_ref, key_ref, value_ref)):
        for head in range(heads):
            first = (3 * head + which) * rows
            columns = slice(head * D_HEAD, (head + 1) * D_HEAD)
            ref[:, columns] = received[first : first + rows].astype(jnp.bfloat16)


def places():
    blk_size, ulysses_size = lax.axis_size("blk"), lax.axis_size("ulysses")
    index = np.arange(blk_size * ulysses_size)
    if blk_size % 2 == 0 and ulysses_size % 2 == 0:
        index = index.reshape(blk_size // 2, 2, ulysses_size // 2, 2).transpose(1, 3, 2, 0)
    return [[int(device) for device in index.reshape(-1)]]


def exchange(chunks):
    return lax.all_to_all(
        chunks, AXES, split_axis=0, concat_axis=0, tiled=True, axis_index_groups=places()
    )


def by_head(queries, key_vectors, value_vectors, cotangent):
    rows = queries.shape[0]
    packed = pl.pallas_call(
        pack_kernel,
        out_shape=jax.ShapeDtypeStruct((HEADS, 4 * rows, D_HEAD), jnp.bfloat16),
        in_specs=[HBM] * 4,
        out_specs=VMEM,
        scratch_shapes=[
            pltpu.VMEM((4,) + queries.shape, jnp.bfloat16),
            pltpu.SemaphoreType.DMA((4,)),
        ],
        compiler_params=PARAMS,
    )(
        *(
            pltpu.with_memory_space_constraint(array, pltpu.HBM)
            for array in (queries, key_vectors, value_vectors, cotangent)
        )
    )
    held = exchange(packed)
    grads = jax.ShapeDtypeStruct((HEADS * 3 * rows, D_HEAD), jnp.bfloat16)
    back = pl.pallas_call(
        lambda *refs: head_kernel(rows, *refs),
        out_shape=grads,
        in_specs=[VMEM],
        out_specs=VMEM,
        compiler_params=PARAMS,
    )(held)
    pair = math.gcd(rows, 2)
    back = exchange(back.reshape(HEADS, 3 * rows // pair, pair, D_HEAD))
    out = jax.ShapeDtypeStruct(queries.shape, jnp.bfloat16)
    return pl.pallas_call(
        unpack_kernel,
        out_shape=(out,) * 3,
        in_specs=[VMEM],
        out_specs=(VMEM,) * 3,
        compiler_params=PARAMS,
    )(back.reshape(grads.shape))


def scores(query_part, key_part, score_scale):
    return (
        jnp.einsum("qhd,khd->hqk", query_part, key_part, preferred_element_type=jnp.float32)
        * score_scale
    )


def by_block(queries, key_vectors, value_vectors, cotangent):
    ulysses_size = lax.axis_size("ulysses")
    head_dev = HEADS // ulysses_size
    score_scale = 1.0 / math.sqrt(D_HEAD)
    query_heads, key_heads, value_heads, grad_heads = (
        lax.all_to_all(queries, "ulysses", split_axis=1, concat_axis=0, tiled=True),
        lax.all_to_all(key_vectors, "ulysses", split_axis=1, concat_axis=0, tiled=True),
        lax.all_to_all(value_vectors, "ulysses", split_axis=1, concat_axis=0, tiled=True),
        lax.all_to_all(cotangent, "ulysses", split_axis=1, concat_axis=0, tiled=True),
    )
    local_rows = query_heads.shape[0]

    def split_heads(matrix):
        return matrix.reshape(matrix.shape[0], head_dev, D_HEAD)

    own_query = split_heads(query_heads)
    own_key = split_heads(key_heads)
    own_value = split_heads(value_heads)
    own_grad = split_heads(grad_heads)
    held_key, held_value = (
        lax.all_gather(key_heads, "blk", axis=0, tiled=True),
        lax.all_gather(value_heads, "blk", axis=0, tiled=True),
    )
    held_key = split_heads(held_key)
    held_value = split_heads(held_value)
    logits = scores(own_query, held_key, score_scale)
    grad_weights = jnp.einsum(
        "qhd,khd->hqk", own_grad, held_value, preferred_element_type=jnp.float32
    )
    block_top = jnp.max(logits, axis=2)
    exp_terms = jnp.exp(logits - block_top[:, :, None])
    row_total = jnp.sum(exp_terms, axis=2)
    row_sum = jnp.sum(exp_terms * grad_weights, axis=2)
    log_total = block_top + jnp.log(row_total)
    row_dot = row_sum / row_total
    all_log, all_dot = (
        lax.all_gather(log_total.T, "blk", axis=0, tiled=True),
        lax.all_gather(row_dot.T, "blk", axis=0, tiled=True),
    )
    logits = scores(own_query, held_key, score_scale)
    weights = jnp.exp(logits - log_total[:, :, None])
    grad_weights = jnp.einsum(
        "qhd,khd->hqk", own_grad, held_value, preferred_element_type=jnp.float32
    )
    grad_low = (weights * (grad_weights - row_dot[:, :, None])).astype(jnp.bfloat16)
    grad_query = jnp.einsum("hqk,khd->qhd", grad_low, held_key, preferred_element_type=jnp.float32)
    remote_query = split_heads(lax.all_gather(query_heads, "blk", axis=0, tiled=True))
    remote_grad = split_heads(lax.all_gather(grad_heads, "blk", axis=0, tiled=True))
    logits = scores(remote_query, own_key, score_scale)
    weights = jnp.exp(logits - all_log.T[:, :, None])
    grad_weights = jnp.einsum(
        "qhd,khd->hqk", remote_grad, own_value, preferred_element_type=jnp.float32
    )
    grad_low = (weights * (grad_weights - all_dot.T[:, :, None])).astype(jnp.bfloat16)
    weights_low = weights.astype(jnp.bfloat16)
    grad_key = jnp.einsum(
        "hqk,qhd->khd", grad_low, remote_query, preferred_element_type=jnp.float32
    )
    grad_value = jnp.einsum(
        "hqk,qhd->khd", weights_low, remote_grad, preferred_element_type=jnp.float32
    )
    grad_key, grad_value = (grad_key, grad_value)

    def to_rows(summed, factor):
        return (summed * factor).astype(jnp.bfloat16).reshape(local_rows, head_dev * D_HEAD)

    return (
        lax.all_to_all(
            to_rows(grad_query, score_scale), "ulysses", split_axis=0, concat_axis=1, tiled=True
        ),
        lax.all_to_all(
            to_rows(grad_key, score_scale), "ulysses", split_axis=0, concat_axis=1, tiled=True
        ),
        lax.all_to_all(
            to_rows(grad_value, 1.0), "ulysses", split_axis=0, concat_axis=1, tiled=True
        ),
    )


def solution(mesh):
    placed = (
        P(("blk", "ulysses"), None),
        P(("blk", "ulysses"), None),
        P(("blk", "ulysses"), None),
        P(("blk", "ulysses"), None),
    )
    local = by_head if mesh.size == HEADS else by_block
    return jax.shard_map(
        local,
        mesh=mesh,
        in_specs=placed,
        out_specs=(
            P(("blk", "ulysses"), None),
            P(("blk", "ulysses"), None),
            P(("blk", "ulysses"), None),
        ),
        check_vma=False,
    )
```

```python
import functools
import math

import jax
import jax.numpy as jnp
import numpy as np
from jax import lax
from jax.experimental import pallas as pl
from jax.experimental.pallas import tpu as pltpu
from jax.sharding import PartitionSpec as P

HEADS = 32
D_HEAD = 128
TILE = 8
CORES = 2
AXES = ("blk", "ulysses")
HBM = pl.BlockSpec(memory_space=pltpu.HBM)
VMEM = pl.BlockSpec(memory_space=pltpu.VMEM)
PARAMS = pltpu.CompilerParams(vmem_limit_bytes=8 * 2**20)


def pack_kernel(query_ref, key_ref, value_ref, grad_ref, out_ref, held, arrived):
    copies = [
        pltpu.make_async_copy(ref, held.at[which], arrived.at[which])
        for which, ref in enumerate((query_ref, key_ref, value_ref, grad_ref))
    ]
    for copy in copies:
        copy.start()
    for copy in copies:
        copy.wait()
    third = query_ref.shape[0] // 3
    for head in range(out_ref.shape[0]):
        columns = slice(head * D_HEAD, (head + 1) * D_HEAD)
        *tops, grad = (held[which, :, columns].astype(jnp.float32) for which in range(4))
        parts = []
        for which, top in enumerate(tops):
            parts += [top, grad[which * third : (which + 1) * third]]
        out_ref[head] = jnp.concatenate(parts, axis=0).astype(jnp.bfloat16)


def dot(left, right, left_dim, right_dim):
    return lax.dot_general(
        left, right, (((left_dim,), (right_dim,)), ((), ())), preferred_element_type=jnp.float32
    )


def head_kernel(rows, places, own_ref, other_ref, out_ref):
    senders = own_ref.shape[0]
    heads = own_ref.shape[1] // (3 * TILE)
    third = rows // 3
    half = senders * TILE
    score_scale = 1.0 / math.sqrt(D_HEAD)
    blocks = [
        ref[sender].astype(jnp.float32)
        for ref in (own_ref, other_ref)
        for sender in range(senders)
    ]
    row = lax.broadcasted_iota(jnp.int32, (TILE, D_HEAD), 0)
    is_key = lax.broadcasted_iota(jnp.int32, (2 * half, 2 * half), 0) % TILE < rows
    grads = []
    for head in range(heads):
        tiles = [[], [], [], []]
        for block in blocks:
            grad = jnp.zeros((TILE, D_HEAD), jnp.float32)
            for which in range(3):
                first = (3 * head + which) * TILE
                tile = block[first : first + TILE]
                tiles[which].append(tile)
                moved = pltpu.roll(tile, (which * third - rows) % TILE, 0)
                inside = (row >= which * third) & (row < (which + 1) * third)
                grad = jnp.where(inside, moved, grad)
            tiles[3].append(grad)
        query, key, value, grad = (
            jnp.concatenate(parts, axis=0).astype(jnp.bfloat16) for parts in tiles
        )
        logits = jnp.where(is_key, dot(key, query, 1, 1), -jnp.inf)
        grad_weights = dot(value, grad, 1, 1)
        top = jnp.max(logits, axis=0, keepdims=True)
        terms = jnp.exp((logits - top) * score_scale)
        inverse = 1.0 / jnp.sum(terms, axis=0, keepdims=True)
        row_dot = jnp.sum(terms * grad_weights, axis=0, keepdims=True) * inverse
        weights = terms * inverse
        grad_low = (weights * (grad_weights - row_dot)).astype(jnp.bfloat16)
        weights_low = weights.astype(jnp.bfloat16)
        grads += [
            dot(grad_low[:, :half], key, 0, 0) * score_scale,
            dot(grad_low[:half], query, 1, 0) * score_scale,
            dot(weights_low[:half], grad, 1, 0),
        ]
    out_ref[...] = jnp.concatenate(
        [
            total[sender * TILE : sender * TILE + rows]
            for sender in places
            for total in grads
        ],
        axis=0,
    ).astype(jnp.bfloat16)


def unpack_kernel(places, in_ref, query_ref, key_ref, value_ref):
    rows = query_ref.shape[0]
    heads = in_ref.shape[0] // (3 * rows)
    received = in_ref[...].astype(jnp.float32)
    for which, ref in enumerate((query_ref, key_ref, value_ref)):
        for place in range(heads):
            first = (3 * place + which) * rows
            head = CORES * places[place // CORES] + place % CORES
            columns = slice(head * D_HEAD, (head + 1) * D_HEAD)
            ref[:, columns] = received[first : first + rows].astype(jnp.bfloat16)


def chip_orders():
    chips = HEADS // CORES
    first = 11 * chips // 16
    inward = [first] + [chip for chip in reversed(range(chips)) if chip != first]
    columns = [int(chip) for chip in np.arange(chips).reshape(-1, 4).T.reshape(-1)]
    turn = columns.index(first)
    return inward, columns[turn:] + columns[:turn]


def exchange(chunks, order):
    groups = [[CORES * chip + core for chip in order] for core in range(CORES)]
    return lax.all_to_all(
        chunks, AXES, split_axis=0, concat_axis=0, tiled=True, axis_index_groups=groups
    )


def by_head(queries, key_vectors, value_vectors, cotangent):
    rows = queries.shape[0]
    if 4 * rows != 3 * TILE:
        return by_block(queries, key_vectors, value_vectors, cotangent)
    chips = HEADS // CORES
    inward, outward = chip_orders()
    places = [inward.index(chip) for chip in outward]
    packed = pl.pallas_call(
        pack_kernel,
        out_shape=jax.ShapeDtypeStruct((HEADS, 4 * rows, D_HEAD), jnp.bfloat16),
        in_specs=[HBM] * 4,
        out_specs=VMEM,
        scratch_shapes=[
            pltpu.VMEM((4,) + queries.shape, jnp.bfloat16),
            pltpu.SemaphoreType.DMA((4,)),
        ],
        compiler_params=PARAMS,
    )(
        *(
            pltpu.with_memory_space_constraint(array, pltpu.HBM)
            for array in (queries, key_vectors, value_vectors, cotangent)
        )
    )
    own = exchange(packed.reshape(chips, CORES * 4 * rows, D_HEAD), inward)
    other = lax.ppermute(own, AXES, [(device, device ^ 1) for device in range(HEADS)])
    grads = jax.ShapeDtypeStruct((HEADS * 3 * rows, D_HEAD), jnp.bfloat16)
    back = pl.pallas_call(
        functools.partial(head_kernel, rows, places),
        out_shape=grads,
        in_specs=[VMEM] * 2,
        out_specs=VMEM,
        compiler_params=PARAMS,
    )(own, other)
    back = exchange(back.reshape(chips, CORES * 3 * rows // 2, 2, D_HEAD), outward)
    out = jax.ShapeDtypeStruct(queries.shape, jnp.bfloat16)
    return pl.pallas_call(
        functools.partial(unpack_kernel, places),
        out_shape=(out,) * 3,
        in_specs=[VMEM],
        out_specs=(VMEM,) * 3,
        compiler_params=PARAMS,
    )(back.reshape(grads.shape))


def scores(query_part, key_part, score_scale):
    return (
        jnp.einsum("qhd,khd->hqk", query_part, key_part, preferred_element_type=jnp.float32)
        * score_scale
    )


def by_block(queries, key_vectors, value_vectors, cotangent):
    ulysses_size = lax.axis_size("ulysses")
    head_dev = HEADS // ulysses_size
    score_scale = 1.0 / math.sqrt(D_HEAD)
    query_heads, key_heads, value_heads, grad_heads = (
        lax.all_to_all(queries, "ulysses", split_axis=1, concat_axis=0, tiled=True),
        lax.all_to_all(key_vectors, "ulysses", split_axis=1, concat_axis=0, tiled=True),
        lax.all_to_all(value_vectors, "ulysses", split_axis=1, concat_axis=0, tiled=True),
        lax.all_to_all(cotangent, "ulysses", split_axis=1, concat_axis=0, tiled=True),
    )
    local_rows = query_heads.shape[0]

    def split_heads(matrix):
        return matrix.reshape(matrix.shape[0], head_dev, D_HEAD)

    own_query = split_heads(query_heads)
    own_key = split_heads(key_heads)
    own_value = split_heads(value_heads)
    own_grad = split_heads(grad_heads)
    held_key, held_value = (
        lax.all_gather(key_heads, "blk", axis=0, tiled=True),
        lax.all_gather(value_heads, "blk", axis=0, tiled=True),
    )
    held_key = split_heads(held_key)
    held_value = split_heads(held_value)
    logits = scores(own_query, held_key, score_scale)
    grad_weights = jnp.einsum(
        "qhd,khd->hqk", own_grad, held_value, preferred_element_type=jnp.float32
    )
    block_top = jnp.max(logits, axis=2)
    exp_terms = jnp.exp(logits - block_top[:, :, None])
    row_total = jnp.sum(exp_terms, axis=2)
    row_sum = jnp.sum(exp_terms * grad_weights, axis=2)
    log_total = block_top + jnp.log(row_total)
    row_dot = row_sum / row_total
    all_log, all_dot = (
        lax.all_gather(log_total.T, "blk", axis=0, tiled=True),
        lax.all_gather(row_dot.T, "blk", axis=0, tiled=True),
    )
    logits = scores(own_query, held_key, score_scale)
    weights = jnp.exp(logits - log_total[:, :, None])
    grad_weights = jnp.einsum(
        "qhd,khd->hqk", own_grad, held_value, preferred_element_type=jnp.float32
    )
    grad_low = (weights * (grad_weights - row_dot[:, :, None])).astype(jnp.bfloat16)
    grad_query = jnp.einsum("hqk,khd->qhd", grad_low, held_key, preferred_element_type=jnp.float32)
    remote_query = split_heads(lax.all_gather(query_heads, "blk", axis=0, tiled=True))
    remote_grad = split_heads(lax.all_gather(grad_heads, "blk", axis=0, tiled=True))
    logits = scores(remote_query, own_key, score_scale)
    weights = jnp.exp(logits - all_log.T[:, :, None])
    grad_weights = jnp.einsum(
        "qhd,khd->hqk", remote_grad, own_value, preferred_element_type=jnp.float32
    )
    grad_low = (weights * (grad_weights - all_dot.T[:, :, None])).astype(jnp.bfloat16)
    weights_low = weights.astype(jnp.bfloat16)
    grad_key = jnp.einsum(
        "hqk,qhd->khd", grad_low, remote_query, preferred_element_type=jnp.float32
    )
    grad_value = jnp.einsum(
        "hqk,qhd->khd", weights_low, remote_grad, preferred_element_type=jnp.float32
    )
    grad_key, grad_value = (grad_key, grad_value)

    def to_rows(summed, factor):
        return (summed * factor).astype(jnp.bfloat16).reshape(local_rows, head_dev * D_HEAD)

    return (
        lax.all_to_all(
            to_rows(grad_query, score_scale), "ulysses", split_axis=0, concat_axis=1, tiled=True
        ),
        lax.all_to_all(
            to_rows(grad_key, score_scale), "ulysses", split_axis=0, concat_axis=1, tiled=True
        ),
        lax.all_to_all(
            to_rows(grad_value, 1.0), "ulysses", split_axis=0, concat_axis=1, tiled=True
        ),
    )


def solution(mesh):
    placed = (
        P(("blk", "ulysses"), None),
        P(("blk", "ulysses"), None),
        P(("blk", "ulysses"), None),
        P(("blk", "ulysses"), None),
    )
    by_heads = mesh.size == HEADS and mesh.shape["ulysses"] % CORES == 0
    local = by_head if by_heads else by_block
    return jax.shard_map(
        local,
        mesh=mesh,
        in_specs=placed,
        out_specs=(
            P(("blk", "ulysses"), None),
            P(("blk", "ulysses"), None),
            P(("blk", "ulysses"), None),
        ),
        check_vma=False,
    )
```

```python
import functools
import math

import jax
import jax.numpy as jnp
import numpy as np
from jax import lax
from jax.experimental import pallas as pl
from jax.experimental.pallas import tpu as pltpu
from jax.sharding import PartitionSpec as P

HEADS = 32
D_HEAD = 128
TILE = 8
CORES = 2
AXES = ("blk", "ulysses")
INWARD = (11, 10, 9, 12, 5, 7, 4, 6, 3, 2, 1, 0, 15, 8, 13, 14)
OUTWARD = (11, 15, 0, 4, 14, 10, 2, 6, 13, 9, 5, 1, 12, 8, 3, 7)
TURNED = (0, 1)
HBM = pl.BlockSpec(memory_space=pltpu.HBM)
VMEM = pl.BlockSpec(memory_space=pltpu.VMEM)
PARAMS = pltpu.CompilerParams(vmem_limit_bytes=8 * 2**20)


def pack_kernel(query_ref, key_ref, value_ref, grad_ref, out_ref, held, arrived):
    copies = [
        pltpu.make_async_copy(ref, held.at[which], arrived.at[which])
        for which, ref in enumerate((query_ref, key_ref, value_ref, grad_ref))
    ]
    for copy in copies:
        copy.start()
    for copy in copies:
        copy.wait()
    third = query_ref.shape[0] // 3
    for head in range(out_ref.shape[0]):
        columns = slice(head * D_HEAD, (head + 1) * D_HEAD)
        *tops, grad = (held[which, :, columns].astype(jnp.float32) for which in range(4))
        parts = []
        for which, top in enumerate(tops):
            parts += [top, grad[which * third : (which + 1) * third]]
        out_ref[head] = jnp.concatenate(parts, axis=0).astype(jnp.bfloat16)


def dot(left, right, left_dim, right_dim):
    return lax.dot_general(
        left, right, (((left_dim,), (right_dim,)), ((), ())), preferred_element_type=jnp.float32
    )


def head_kernel(rows, places, own_ref, other_ref, out_ref):
    senders = own_ref.shape[0]
    heads = own_ref.shape[1] // (3 * TILE)
    third = rows // 3
    half = senders * TILE
    score_scale = 1.0 / math.sqrt(D_HEAD)
    blocks = [
        ref[sender].astype(jnp.float32)
        for ref in (own_ref, other_ref)
        for sender in range(senders)
    ]
    row = lax.broadcasted_iota(jnp.int32, (TILE, D_HEAD), 0)
    is_key = lax.broadcasted_iota(jnp.int32, (2 * half, 2 * half), 0) % TILE < rows
    grads = []
    for head in range(heads):
        tiles = [[], [], [], []]
        for block in blocks:
            grad = jnp.zeros((TILE, D_HEAD), jnp.float32)
            for which in range(3):
                first = (3 * head + which) * TILE
                tile = block[first : first + TILE]
                tiles[which].append(tile)
                moved = pltpu.roll(tile, (which * third - rows) % TILE, 0)
                inside = (row >= which * third) & (row < (which + 1) * third)
                grad = jnp.where(inside, moved, grad)
            tiles[3].append(grad)
        query, key, value, grad = (
            jnp.concatenate(parts, axis=0).astype(jnp.bfloat16) for parts in tiles
        )
        logits = jnp.where(is_key, dot(key, query, 1, 1), -jnp.inf)
        grad_weights = dot(value, grad, 1, 1)
        top = jnp.max(logits, axis=0, keepdims=True)
        terms = jnp.exp((logits - top) * score_scale)
        inverse = 1.0 / jnp.sum(terms, axis=0, keepdims=True)
        row_dot = jnp.sum(terms * grad_weights, axis=0, keepdims=True) * inverse
        weights = terms * inverse
        grad_low = (weights * (grad_weights - row_dot)).astype(jnp.bfloat16)
        weights_low = weights.astype(jnp.bfloat16)
        grads += [
            dot(grad_low[:, :half], key, 0, 0) * score_scale,
            dot(grad_low[:half], query, 1, 0) * score_scale,
            dot(weights_low[:half], grad, 1, 0),
        ]
    out_ref[...] = jnp.concatenate(
        [
            total[sender * TILE : sender * TILE + rows]
            for sender in places
            for total in grads
        ],
        axis=0,
    ).astype(jnp.bfloat16)


def unpack_kernel(places, in_ref, query_ref, key_ref, value_ref):
    rows = query_ref.shape[0]
    heads = in_ref.shape[0] // (3 * rows)
    received = in_ref[...].astype(jnp.float32)
    for which, ref in enumerate((query_ref, key_ref, value_ref)):
        for place in range(heads):
            first = (3 * place + which) * rows
            head = CORES * places[place // CORES] + place % CORES
            columns = slice(head * D_HEAD, (head + 1) * D_HEAD)
            ref[:, columns] = received[first : first + rows].astype(jnp.bfloat16)


def exchange(chunks, order):
    groups = [
        [CORES * chip + (core ^ (chip in TURNED)) for chip in order] for core in range(CORES)
    ]
    return lax.all_to_all(
        chunks, AXES, split_axis=0, concat_axis=0, tiled=True, axis_index_groups=groups
    )


def by_head(queries, key_vectors, value_vectors, cotangent):
    rows = queries.shape[0]
    if 4 * rows != 3 * TILE:
        return by_block(queries, key_vectors, value_vectors, cotangent)
    chips = HEADS // CORES
    places = [INWARD.index(chip) for chip in OUTWARD]
    packed = pl.pallas_call(
        pack_kernel,
        out_shape=jax.ShapeDtypeStruct((HEADS, 4 * rows, D_HEAD), jnp.bfloat16),
        in_specs=[HBM] * 4,
        out_specs=VMEM,
        scratch_shapes=[
            pltpu.VMEM((4,) + queries.shape, jnp.bfloat16),
            pltpu.SemaphoreType.DMA((4,)),
        ],
        compiler_params=PARAMS,
    )(
        *(
            pltpu.with_memory_space_constraint(array, pltpu.HBM)
            for array in (queries, key_vectors, value_vectors, cotangent)
        )
    )
    own = exchange(packed.reshape(chips, CORES * 4 * rows, D_HEAD), INWARD)
    other = lax.ppermute(own, AXES, [(device, device ^ 1) for device in range(HEADS)])
    grads = jax.ShapeDtypeStruct((HEADS * 3 * rows, D_HEAD), jnp.bfloat16)
    back = pl.pallas_call(
        functools.partial(head_kernel, rows, places),
        out_shape=grads,
        in_specs=[VMEM] * 2,
        out_specs=VMEM,
        compiler_params=PARAMS,
    )(own, other)
    back = exchange(back.reshape(chips, CORES * 3 * rows // 2, 2, D_HEAD), OUTWARD)
    out = jax.ShapeDtypeStruct(queries.shape, jnp.bfloat16)
    return pl.pallas_call(
        functools.partial(unpack_kernel, places),
        out_shape=(out,) * 3,
        in_specs=[VMEM],
        out_specs=(VMEM,) * 3,
        compiler_params=PARAMS,
    )(back.reshape(grads.shape))


def scores(query_part, key_part, score_scale):
    return (
        jnp.einsum("qhd,khd->hqk", query_part, key_part, preferred_element_type=jnp.float32)
        * score_scale
    )


def by_block(queries, key_vectors, value_vectors, cotangent):
    ulysses_size = lax.axis_size("ulysses")
    head_dev = HEADS // ulysses_size
    score_scale = 1.0 / math.sqrt(D_HEAD)
    query_heads, key_heads, value_heads, grad_heads = (
        lax.all_to_all(queries, "ulysses", split_axis=1, concat_axis=0, tiled=True),
        lax.all_to_all(key_vectors, "ulysses", split_axis=1, concat_axis=0, tiled=True),
        lax.all_to_all(value_vectors, "ulysses", split_axis=1, concat_axis=0, tiled=True),
        lax.all_to_all(cotangent, "ulysses", split_axis=1, concat_axis=0, tiled=True),
    )
    local_rows = query_heads.shape[0]

    def split_heads(matrix):
        return matrix.reshape(matrix.shape[0], head_dev, D_HEAD)

    own_query = split_heads(query_heads)
    own_key = split_heads(key_heads)
    own_value = split_heads(value_heads)
    own_grad = split_heads(grad_heads)
    held_key, held_value = (
        lax.all_gather(key_heads, "blk", axis=0, tiled=True),
        lax.all_gather(value_heads, "blk", axis=0, tiled=True),
    )
    held_key = split_heads(held_key)
    held_value = split_heads(held_value)
    logits = scores(own_query, held_key, score_scale)
    grad_weights = jnp.einsum(
        "qhd,khd->hqk", own_grad, held_value, preferred_element_type=jnp.float32
    )
    block_top = jnp.max(logits, axis=2)
    exp_terms = jnp.exp(logits - block_top[:, :, None])
    row_total = jnp.sum(exp_terms, axis=2)
    row_sum = jnp.sum(exp_terms * grad_weights, axis=2)
    log_total = block_top + jnp.log(row_total)
    row_dot = row_sum / row_total
    all_log, all_dot = (
        lax.all_gather(log_total.T, "blk", axis=0, tiled=True),
        lax.all_gather(row_dot.T, "blk", axis=0, tiled=True),
    )
    logits = scores(own_query, held_key, score_scale)
    weights = jnp.exp(logits - log_total[:, :, None])
    grad_weights = jnp.einsum(
        "qhd,khd->hqk", own_grad, held_value, preferred_element_type=jnp.float32
    )
    grad_low = (weights * (grad_weights - row_dot[:, :, None])).astype(jnp.bfloat16)
    grad_query = jnp.einsum("hqk,khd->qhd", grad_low, held_key, preferred_element_type=jnp.float32)
    remote_query = split_heads(lax.all_gather(query_heads, "blk", axis=0, tiled=True))
    remote_grad = split_heads(lax.all_gather(grad_heads, "blk", axis=0, tiled=True))
    logits = scores(remote_query, own_key, score_scale)
    weights = jnp.exp(logits - all_log.T[:, :, None])
    grad_weights = jnp.einsum(
        "qhd,khd->hqk", remote_grad, own_value, preferred_element_type=jnp.float32
    )
    grad_low = (weights * (grad_weights - all_dot.T[:, :, None])).astype(jnp.bfloat16)
    weights_low = weights.astype(jnp.bfloat16)
    grad_key = jnp.einsum(
        "hqk,qhd->khd", grad_low, remote_query, preferred_element_type=jnp.float32
    )
    grad_value = jnp.einsum(
        "hqk,qhd->khd", weights_low, remote_grad, preferred_element_type=jnp.float32
    )
    grad_key, grad_value = (grad_key, grad_value)

    def to_rows(summed, factor):
        return (summed * factor).astype(jnp.bfloat16).reshape(local_rows, head_dev * D_HEAD)

    return (
        lax.all_to_all(
            to_rows(grad_query, score_scale), "ulysses", split_axis=0, concat_axis=1, tiled=True
        ),
        lax.all_to_all(
            to_rows(grad_key, score_scale), "ulysses", split_axis=0, concat_axis=1, tiled=True
        ),
        lax.all_to_all(
            to_rows(grad_value, 1.0), "ulysses", split_axis=0, concat_axis=1, tiled=True
        ),
    )


def solution(mesh):
    placed = (
        P(("blk", "ulysses"), None),
        P(("blk", "ulysses"), None),
        P(("blk", "ulysses"), None),
        P(("blk", "ulysses"), None),
    )
    by_heads = mesh.size == HEADS == CORES * len(INWARD) and mesh.shape["ulysses"] % CORES == 0
    local = by_head if by_heads else by_block
    return jax.shard_map(
        local,
        mesh=mesh,
        in_specs=placed,
        out_specs=(
            P(("blk", "ulysses"), None),
            P(("blk", "ulysses"), None),
            P(("blk", "ulysses"), None),
        ),
        check_vma=False,
    )
```

```python
import functools
import math

import jax
import jax.numpy as jnp
from jax import lax
from jax.experimental import pallas as pl
from jax.experimental.pallas import tpu as pltpu
from jax.sharding import PartitionSpec as P

HEADS = 32
D_HEAD = 128
TILE = 8
CORES = 2
AXES = ("blk", "ulysses")
INWARD = (11, 10, 9, 5, 7, 4, 6, 3, 2, 1, 0, 15, 8, 12, 13, 14)
OUTWARD = (11, 15, 0, 4, 14, 9, 2, 6, 13, 10, 3, 1, 12, 8, 5, 7)
TURNED = (0, 1)
HBM = pl.BlockSpec(memory_space=pltpu.HBM)
VMEM = pl.BlockSpec(memory_space=pltpu.VMEM)
PARAMS = pltpu.CompilerParams(vmem_limit_bytes=8 * 2**20)


def pack_kernel(query_ref, key_ref, value_ref, grad_ref, out_ref, held, arrived):
    copies = [
        pltpu.make_async_copy(ref, held.at[which], arrived.at[which])
        for which, ref in enumerate((query_ref, key_ref, value_ref, grad_ref))
    ]
    for copy in copies:
        copy.start()
    for copy in copies:
        copy.wait()
    third = query_ref.shape[0] // 3
    for head in range(out_ref.shape[0]):
        columns = slice(head * D_HEAD, (head + 1) * D_HEAD)
        *tops, grad = (held[which, :, columns].astype(jnp.float32) for which in range(4))
        parts = []
        for which, top in enumerate(tops):
            parts += [top, grad[which * third : (which + 1) * third]]
        out_ref[head] = jnp.concatenate(parts, axis=0).astype(jnp.bfloat16)


def dot(left, right, left_dim, right_dim):
    return lax.dot_general(
        left, right, (((left_dim,), (right_dim,)), ((), ())), preferred_element_type=jnp.float32
    )


def head_kernel(rows, places, own_ref, other_ref, out_ref):
    senders = own_ref.shape[0]
    heads = own_ref.shape[1] // (3 * TILE)
    third = rows // 3
    half = senders * TILE
    score_scale = 1.0 / math.sqrt(D_HEAD)
    blocks = [
        ref[sender].astype(jnp.float32)
        for ref in (own_ref, other_ref)
        for sender in range(senders)
    ]
    row = lax.broadcasted_iota(jnp.int32, (TILE, D_HEAD), 0)
    is_key = lax.broadcasted_iota(jnp.int32, (2 * half, 2 * half), 0) % TILE < rows
    grads = []
    for head in range(heads):
        tiles = [[], [], [], []]
        for block in blocks:
            grad = jnp.zeros((TILE, D_HEAD), jnp.float32)
            for which in range(3):
                first = (3 * head + which) * TILE
                tile = block[first : first + TILE]
                tiles[which].append(tile)
                moved = pltpu.roll(tile, (which * third - rows) % TILE, 0)
                inside = (row >= which * third) & (row < (which + 1) * third)
                grad = jnp.where(inside, moved, grad)
            tiles[3].append(grad)
        query, key, value, grad = (
            jnp.concatenate(parts, axis=0).astype(jnp.bfloat16) for parts in tiles
        )
        logits = jnp.where(is_key, dot(key, query, 1, 1), -jnp.inf)
        grad_weights = dot(value, grad, 1, 1)
        top = jnp.max(logits, axis=0, keepdims=True)
        terms = jnp.exp((logits - top) * score_scale)
        inverse = 1.0 / jnp.sum(terms, axis=0, keepdims=True)
        row_dot = jnp.sum(terms * grad_weights, axis=0, keepdims=True) * inverse
        weights = terms * inverse
        grad_low = (weights * (grad_weights - row_dot)).astype(jnp.bfloat16)
        weights_low = weights.astype(jnp.bfloat16)
        grads += [
            dot(grad_low[:, :half], key, 0, 0) * score_scale,
            dot(grad_low[:half], query, 1, 0) * score_scale,
            dot(weights_low[:half], grad, 1, 0),
        ]
    out_ref[...] = jnp.concatenate(
        [
            total[sender * TILE : sender * TILE + rows]
            for sender in places
            for total in grads
        ],
        axis=0,
    ).astype(jnp.bfloat16)


def unpack_kernel(places, in_ref, query_ref, key_ref, value_ref):
    rows = query_ref.shape[0]
    heads = in_ref.shape[0] // (3 * rows)
    received = in_ref[...].astype(jnp.float32)
    for which, ref in enumerate((query_ref, key_ref, value_ref)):
        for place in range(heads):
            first = (3 * place + which) * rows
            head = CORES * places[place // CORES] + place % CORES
            columns = slice(head * D_HEAD, (head + 1) * D_HEAD)
            ref[:, columns] = received[first : first + rows].astype(jnp.bfloat16)


def exchange(chunks, order):
    groups = [
        [CORES * chip + (core ^ (chip in TURNED)) for chip in order] for core in range(CORES)
    ]
    return lax.all_to_all(
        chunks, AXES, split_axis=0, concat_axis=0, tiled=True, axis_index_groups=groups
    )


def by_head(queries, key_vectors, value_vectors, cotangent):
    rows = queries.shape[0]
    if 4 * rows != 3 * TILE:
        return by_block(queries, key_vectors, value_vectors, cotangent)
    chips = HEADS // CORES
    places = [INWARD.index(chip) for chip in OUTWARD]
    packed = pl.pallas_call(
        pack_kernel,
        out_shape=jax.ShapeDtypeStruct((HEADS, 4 * rows, D_HEAD), jnp.bfloat16),
        in_specs=[HBM] * 4,
        out_specs=VMEM,
        scratch_shapes=[
            pltpu.VMEM((4,) + queries.shape, jnp.bfloat16),
            pltpu.SemaphoreType.DMA((4,)),
        ],
        compiler_params=PARAMS,
    )(
        *(
            pltpu.with_memory_space_constraint(array, pltpu.HBM)
            for array in (queries, key_vectors, value_vectors, cotangent)
        )
    )
    own = exchange(packed.reshape(chips, CORES * 4 * rows, D_HEAD), INWARD)
    other = lax.ppermute(own, AXES, [(device, device ^ 1) for device in range(HEADS)])
    grads = jax.ShapeDtypeStruct((HEADS * 3 * rows, D_HEAD), jnp.bfloat16)
    back = pl.pallas_call(
        functools.partial(head_kernel, rows, places),
        out_shape=grads,
        in_specs=[VMEM] * 2,
        out_specs=VMEM,
        compiler_params=PARAMS,
    )(own, other)
    back = exchange(back.reshape(chips, CORES * 3 * rows // 2, 2, D_HEAD), OUTWARD)
    out = jax.ShapeDtypeStruct(queries.shape, jnp.bfloat16)
    return pl.pallas_call(
        functools.partial(unpack_kernel, places),
        out_shape=(out,) * 3,
        in_specs=[VMEM],
        out_specs=(VMEM,) * 3,
        compiler_params=PARAMS,
    )(back.reshape(grads.shape))


def scores(query_part, key_part, score_scale):
    return (
        jnp.einsum("qhd,khd->hqk", query_part, key_part, preferred_element_type=jnp.float32)
        * score_scale
    )


def by_block(queries, key_vectors, value_vectors, cotangent):
    ulysses_size = lax.axis_size("ulysses")
    head_dev = HEADS // ulysses_size
    score_scale = 1.0 / math.sqrt(D_HEAD)
    query_heads, key_heads, value_heads, grad_heads = (
        lax.all_to_all(queries, "ulysses", split_axis=1, concat_axis=0, tiled=True),
        lax.all_to_all(key_vectors, "ulysses", split_axis=1, concat_axis=0, tiled=True),
        lax.all_to_all(value_vectors, "ulysses", split_axis=1, concat_axis=0, tiled=True),
        lax.all_to_all(cotangent, "ulysses", split_axis=1, concat_axis=0, tiled=True),
    )
    local_rows = query_heads.shape[0]

    def split_heads(matrix):
        return matrix.reshape(matrix.shape[0], head_dev, D_HEAD)

    own_query = split_heads(query_heads)
    own_key = split_heads(key_heads)
    own_value = split_heads(value_heads)
    own_grad = split_heads(grad_heads)
    held_key, held_value = (
        lax.all_gather(key_heads, "blk", axis=0, tiled=True),
        lax.all_gather(value_heads, "blk", axis=0, tiled=True),
    )
    held_key = split_heads(held_key)
    held_value = split_heads(held_value)
    logits = scores(own_query, held_key, score_scale)
    grad_weights = jnp.einsum(
        "qhd,khd->hqk", own_grad, held_value, preferred_element_type=jnp.float32
    )
    block_top = jnp.max(logits, axis=2)
    exp_terms = jnp.exp(logits - block_top[:, :, None])
    row_total = jnp.sum(exp_terms, axis=2)
    row_sum = jnp.sum(exp_terms * grad_weights, axis=2)
    log_total = block_top + jnp.log(row_total)
    row_dot = row_sum / row_total
    all_log, all_dot = (
        lax.all_gather(log_total.T, "blk", axis=0, tiled=True),
        lax.all_gather(row_dot.T, "blk", axis=0, tiled=True),
    )
    logits = scores(own_query, held_key, score_scale)
    weights = jnp.exp(logits - log_total[:, :, None])
    grad_weights = jnp.einsum(
        "qhd,khd->hqk", own_grad, held_value, preferred_element_type=jnp.float32
    )
    grad_low = (weights * (grad_weights - row_dot[:, :, None])).astype(jnp.bfloat16)
    grad_query = jnp.einsum("hqk,khd->qhd", grad_low, held_key, preferred_element_type=jnp.float32)
    remote_query = split_heads(lax.all_gather(query_heads, "blk", axis=0, tiled=True))
    remote_grad = split_heads(lax.all_gather(grad_heads, "blk", axis=0, tiled=True))
    logits = scores(remote_query, own_key, score_scale)
    weights = jnp.exp(logits - all_log.T[:, :, None])
    grad_weights = jnp.einsum(
        "qhd,khd->hqk", remote_grad, own_value, preferred_element_type=jnp.float32
    )
    grad_low = (weights * (grad_weights - all_dot.T[:, :, None])).astype(jnp.bfloat16)
    weights_low = weights.astype(jnp.bfloat16)
    grad_key = jnp.einsum(
        "hqk,qhd->khd", grad_low, remote_query, preferred_element_type=jnp.float32
    )
    grad_value = jnp.einsum(
        "hqk,qhd->khd", weights_low, remote_grad, preferred_element_type=jnp.float32
    )
    grad_key, grad_value = (grad_key, grad_value)

    def to_rows(summed, factor):
        return (summed * factor).astype(jnp.bfloat16).reshape(local_rows, head_dev * D_HEAD)

    return (
        lax.all_to_all(
            to_rows(grad_query, score_scale), "ulysses", split_axis=0, concat_axis=1, tiled=True
        ),
        lax.all_to_all(
            to_rows(grad_key, score_scale), "ulysses", split_axis=0, concat_axis=1, tiled=True
        ),
        lax.all_to_all(
            to_rows(grad_value, 1.0), "ulysses", split_axis=0, concat_axis=1, tiled=True
        ),
    )


def solution(mesh):
    placed = (
        P(("blk", "ulysses"), None),
        P(("blk", "ulysses"), None),
        P(("blk", "ulysses"), None),
        P(("blk", "ulysses"), None),
    )
    by_heads = mesh.size == HEADS == CORES * len(INWARD) and mesh.shape["ulysses"] % CORES == 0
    local = by_head if by_heads else by_block
    return jax.shard_map(
        local,
        mesh=mesh,
        in_specs=placed,
        out_specs=(
            P(("blk", "ulysses"), None),
            P(("blk", "ulysses"), None),
            P(("blk", "ulysses"), None),
        ),
        check_vma=False,
    )
```

```python
import functools
import math

import jax
import jax.numpy as jnp
from jax import lax
from jax.experimental import pallas as pl
from jax.experimental.pallas import tpu as pltpu
from jax.sharding import PartitionSpec as P

HEADS = 32
D_HEAD = 128
TILE = 8
CORES = 2
AXES = ("blk", "ulysses")
INWARD = (11, 10, 9, 5, 7, 4, 6, 3, 2, 1, 0, 15, 8, 12, 13, 14)
OUTWARD = (11, 15, 0, 4, 14, 7, 5, 8, 12, 2, 3, 10, 13, 6, 1, 9)
TURNED = (0, 1)
HBM = pl.BlockSpec(memory_space=pltpu.HBM)
VMEM = pl.BlockSpec(memory_space=pltpu.VMEM)
PARAMS = pltpu.CompilerParams(vmem_limit_bytes=8 * 2**20)


def pack_kernel(query_ref, key_ref, value_ref, grad_ref, out_ref, held, arrived):
    copies = [
        pltpu.make_async_copy(ref, held.at[which], arrived.at[which])
        for which, ref in enumerate((query_ref, key_ref, value_ref, grad_ref))
    ]
    for copy in copies:
        copy.start()
    for copy in copies:
        copy.wait()
    third = query_ref.shape[0] // 3
    for head in range(out_ref.shape[0]):
        columns = slice(head * D_HEAD, (head + 1) * D_HEAD)
        *tops, grad = (held[which, :, columns].astype(jnp.float32) for which in range(4))
        parts = []
        for which, top in enumerate(tops):
            parts += [top, grad[which * third : (which + 1) * third]]
        out_ref[head] = jnp.concatenate(parts, axis=0).astype(jnp.bfloat16)


def dot(left, right, left_dim, right_dim):
    return lax.dot_general(
        left, right, (((left_dim,), (right_dim,)), ((), ())), preferred_element_type=jnp.float32
    )


def head_kernel(rows, places, own_ref, other_ref, out_ref):
    senders = own_ref.shape[0]
    heads = own_ref.shape[1] // (3 * TILE)
    third = rows // 3
    half = senders * TILE
    score_scale = 1.0 / math.sqrt(D_HEAD)
    blocks = [
        ref[sender].astype(jnp.float32)
        for ref in (own_ref, other_ref)
        for sender in range(senders)
    ]
    row = lax.broadcasted_iota(jnp.int32, (TILE, D_HEAD), 0)
    is_key = lax.broadcasted_iota(jnp.int32, (2 * half, 2 * half), 0) % TILE < rows
    grads = []
    for head in range(heads):
        tiles = [[], [], [], []]
        for block in blocks:
            grad = jnp.zeros((TILE, D_HEAD), jnp.float32)
            for which in range(3):
                first = (3 * head + which) * TILE
                tile = block[first : first + TILE]
                tiles[which].append(tile)
                moved = pltpu.roll(tile, (which * third - rows) % TILE, 0)
                inside = (row >= which * third) & (row < (which + 1) * third)
                grad = jnp.where(inside, moved, grad)
            tiles[3].append(grad)
        query, key, value, grad = (
            jnp.concatenate(parts, axis=0).astype(jnp.bfloat16) for parts in tiles
        )
        logits = jnp.where(is_key, dot(key, query, 1, 1), -jnp.inf)
        grad_weights = dot(value, grad, 1, 1)
        top = jnp.max(logits, axis=0, keepdims=True)
        terms = jnp.exp((logits - top) * score_scale)
        inverse = 1.0 / jnp.sum(terms, axis=0, keepdims=True)
        row_dot = jnp.sum(terms * grad_weights, axis=0, keepdims=True) * inverse
        weights = terms * inverse
        grad_low = (weights * (grad_weights - row_dot)).astype(jnp.bfloat16)
        weights_low = weights.astype(jnp.bfloat16)
        grads += [
            dot(grad_low[:, :half], key, 0, 0) * score_scale,
            dot(grad_low[:half], query, 1, 0) * score_scale,
            dot(weights_low[:half], grad, 1, 0),
        ]
    out_ref[...] = jnp.concatenate(
        [
            total[sender * TILE : sender * TILE + rows]
            for sender in places
            for total in grads
        ],
        axis=0,
    ).astype(jnp.bfloat16)


def unpack_kernel(places, in_ref, query_ref, key_ref, value_ref):
    rows = query_ref.shape[0]
    heads = in_ref.shape[0] // (3 * rows)
    received = in_ref[...].astype(jnp.float32)
    for which, ref in enumerate((query_ref, key_ref, value_ref)):
        for place in range(heads):
            first = (3 * place + which) * rows
            head = CORES * places[place // CORES] + place % CORES
            columns = slice(head * D_HEAD, (head + 1) * D_HEAD)
            ref[:, columns] = received[first : first + rows].astype(jnp.bfloat16)


def exchange(chunks, order):
    groups = [
        [CORES * chip + (core ^ (chip in TURNED)) for chip in order] for core in range(CORES)
    ]
    return lax.all_to_all(
        chunks, AXES, split_axis=0, concat_axis=0, tiled=True, axis_index_groups=groups
    )


def by_head(queries, key_vectors, value_vectors, cotangent):
    rows = queries.shape[0]
    if 4 * rows != 3 * TILE:
        return by_block(queries, key_vectors, value_vectors, cotangent)
    chips = HEADS // CORES
    places = [INWARD.index(chip) for chip in OUTWARD]
    packed = pl.pallas_call(
        pack_kernel,
        out_shape=jax.ShapeDtypeStruct((HEADS, 4 * rows, D_HEAD), jnp.bfloat16),
        in_specs=[HBM] * 4,
        out_specs=VMEM,
        scratch_shapes=[
            pltpu.VMEM((4,) + queries.shape, jnp.bfloat16),
            pltpu.SemaphoreType.DMA((4,)),
        ],
        compiler_params=PARAMS,
    )(
        *(
            pltpu.with_memory_space_constraint(array, pltpu.HBM)
            for array in (queries, key_vectors, value_vectors, cotangent)
        )
    )
    own = exchange(packed.reshape(chips, CORES * 4 * rows, D_HEAD), INWARD)
    other = lax.ppermute(own, AXES, [(device, device ^ 1) for device in range(HEADS)])
    grads = jax.ShapeDtypeStruct((HEADS * 3 * rows, D_HEAD), jnp.bfloat16)
    back = pl.pallas_call(
        functools.partial(head_kernel, rows, places),
        out_shape=grads,
        in_specs=[VMEM] * 2,
        out_specs=VMEM,
        compiler_params=PARAMS,
    )(own, other)
    back = exchange(back.reshape(chips, CORES * 3 * rows // 2, 2, D_HEAD), OUTWARD)
    out = jax.ShapeDtypeStruct(queries.shape, jnp.bfloat16)
    return pl.pallas_call(
        functools.partial(unpack_kernel, places),
        out_shape=(out,) * 3,
        in_specs=[VMEM],
        out_specs=(VMEM,) * 3,
        compiler_params=PARAMS,
    )(back.reshape(grads.shape))


def scores(query_part, key_part, score_scale):
    return (
        jnp.einsum("qhd,khd->hqk", query_part, key_part, preferred_element_type=jnp.float32)
        * score_scale
    )


def by_block(queries, key_vectors, value_vectors, cotangent):
    ulysses_size = lax.axis_size("ulysses")
    head_dev = HEADS // ulysses_size
    score_scale = 1.0 / math.sqrt(D_HEAD)
    query_heads, key_heads, value_heads, grad_heads = (
        lax.all_to_all(queries, "ulysses", split_axis=1, concat_axis=0, tiled=True),
        lax.all_to_all(key_vectors, "ulysses", split_axis=1, concat_axis=0, tiled=True),
        lax.all_to_all(value_vectors, "ulysses", split_axis=1, concat_axis=0, tiled=True),
        lax.all_to_all(cotangent, "ulysses", split_axis=1, concat_axis=0, tiled=True),
    )
    local_rows = query_heads.shape[0]

    def split_heads(matrix):
        return matrix.reshape(matrix.shape[0], head_dev, D_HEAD)

    own_query = split_heads(query_heads)
    own_key = split_heads(key_heads)
    own_value = split_heads(value_heads)
    own_grad = split_heads(grad_heads)
    held_key, held_value = (
        lax.all_gather(key_heads, "blk", axis=0, tiled=True),
        lax.all_gather(value_heads, "blk", axis=0, tiled=True),
    )
    held_key = split_heads(held_key)
    held_value = split_heads(held_value)
    logits = scores(own_query, held_key, score_scale)
    grad_weights = jnp.einsum(
        "qhd,khd->hqk", own_grad, held_value, preferred_element_type=jnp.float32
    )
    block_top = jnp.max(logits, axis=2)
    exp_terms = jnp.exp(logits - block_top[:, :, None])
    row_total = jnp.sum(exp_terms, axis=2)
    row_sum = jnp.sum(exp_terms * grad_weights, axis=2)
    log_total = block_top + jnp.log(row_total)
    row_dot = row_sum / row_total
    all_log, all_dot = (
        lax.all_gather(log_total.T, "blk", axis=0, tiled=True),
        lax.all_gather(row_dot.T, "blk", axis=0, tiled=True),
    )
    logits = scores(own_query, held_key, score_scale)
    weights = jnp.exp(logits - log_total[:, :, None])
    grad_weights = jnp.einsum(
        "qhd,khd->hqk", own_grad, held_value, preferred_element_type=jnp.float32
    )
    grad_low = (weights * (grad_weights - row_dot[:, :, None])).astype(jnp.bfloat16)
    grad_query = jnp.einsum("hqk,khd->qhd", grad_low, held_key, preferred_element_type=jnp.float32)
    remote_query = split_heads(lax.all_gather(query_heads, "blk", axis=0, tiled=True))
    remote_grad = split_heads(lax.all_gather(grad_heads, "blk", axis=0, tiled=True))
    logits = scores(remote_query, own_key, score_scale)
    weights = jnp.exp(logits - all_log.T[:, :, None])
    grad_weights = jnp.einsum(
        "qhd,khd->hqk", remote_grad, own_value, preferred_element_type=jnp.float32
    )
    grad_low = (weights * (grad_weights - all_dot.T[:, :, None])).astype(jnp.bfloat16)
    weights_low = weights.astype(jnp.bfloat16)
    grad_key = jnp.einsum(
        "hqk,qhd->khd", grad_low, remote_query, preferred_element_type=jnp.float32
    )
    grad_value = jnp.einsum(
        "hqk,qhd->khd", weights_low, remote_grad, preferred_element_type=jnp.float32
    )
    grad_key, grad_value = (grad_key, grad_value)

    def to_rows(summed, factor):
        return (summed * factor).astype(jnp.bfloat16).reshape(local_rows, head_dev * D_HEAD)

    return (
        lax.all_to_all(
            to_rows(grad_query, score_scale), "ulysses", split_axis=0, concat_axis=1, tiled=True
        ),
        lax.all_to_all(
            to_rows(grad_key, score_scale), "ulysses", split_axis=0, concat_axis=1, tiled=True
        ),
        lax.all_to_all(
            to_rows(grad_value, 1.0), "ulysses", split_axis=0, concat_axis=1, tiled=True
        ),
    )


def solution(mesh):
    placed = (
        P(("blk", "ulysses"), None),
        P(("blk", "ulysses"), None),
        P(("blk", "ulysses"), None),
        P(("blk", "ulysses"), None),
    )
    by_heads = mesh.size == HEADS == CORES * len(INWARD) and mesh.shape["ulysses"] % CORES == 0
    local = by_head if by_heads else by_block
    return jax.shard_map(
        local,
        mesh=mesh,
        in_specs=placed,
        out_specs=(
            P(("blk", "ulysses"), None),
            P(("blk", "ulysses"), None),
            P(("blk", "ulysses"), None),
        ),
        check_vma=False,
    )
```

```python
import functools
import math

import jax
import jax.numpy as jnp
from jax import lax
from jax.experimental import pallas as pl
from jax.experimental.pallas import tpu as pltpu
from jax.sharding import PartitionSpec as P

HEADS = 32
D_HEAD = 128
TILE = 8
CORES = 2
AXES = ("blk", "ulysses")
INWARD = (11, 10, 9, 5, 7, 4, 6, 3, 2, 1, 0, 15, 8, 12, 13, 14)
OUTWARD = (11, 15, 0, 4, 14, 7, 5, 8, 12, 2, 3, 10, 13, 6, 1, 9)
TURNED = (0, 1)
HBM = pl.BlockSpec(memory_space=pltpu.HBM)
VMEM = pl.BlockSpec(memory_space=pltpu.VMEM)
PARAMS = pltpu.CompilerParams(vmem_limit_bytes=8 * 2**20)


def pack_kernel(query_ref, key_ref, value_ref, grad_ref, out_ref, held, arrived):
    rows, columns = query_ref.shape
    halves = [slice(part * columns // 2, (part + 1) * columns // 2) for part in range(2)]
    copies = [
        [
            pltpu.make_async_copy(ref.at[:, half], held.at[which, :, half], arrived.at[part, which])
            for which, ref in enumerate((query_ref, key_ref, value_ref, grad_ref))
        ]
        for part, half in enumerate(halves)
    ]
    for part in copies:
        for copy in part:
            copy.start()
    third = rows // 3
    heads = out_ref.shape[0]
    for part in range(2):
        for copy in copies[part]:
            copy.wait()
        for head in range(part * heads // 2, (part + 1) * heads // 2):
            columns = slice(head * D_HEAD, (head + 1) * D_HEAD)
            *tops, grad = (held[which, :, columns].astype(jnp.float32) for which in range(4))
            parts = []
            for which, top in enumerate(tops):
                parts += [top, grad[which * third : (which + 1) * third]]
            out_ref[head] = jnp.concatenate(parts, axis=0).astype(jnp.bfloat16)


def dot(left, right, left_dim, right_dim):
    return lax.dot_general(
        left, right, (((left_dim,), (right_dim,)), ((), ())), preferred_element_type=jnp.float32
    )


def head_kernel(rows, places, own_ref, other_ref, out_ref):
    senders = own_ref.shape[0]
    heads = own_ref.shape[1] // (3 * TILE)
    third = rows // 3
    half = senders * TILE
    score_scale = 1.0 / math.sqrt(D_HEAD)
    blocks = [
        ref[sender].astype(jnp.float32)
        for ref in (own_ref, other_ref)
        for sender in range(senders)
    ]
    row = lax.broadcasted_iota(jnp.int32, (TILE, D_HEAD), 0)
    is_key = lax.broadcasted_iota(jnp.int32, (2 * half, 2 * half), 0) % TILE < rows
    grads = []
    for head in range(heads):
        first = 3 * head * TILE
        query, key, value = (
            jnp.concatenate(
                [
                    ref[:, first + which * TILE : first + (which + 1) * TILE].reshape(half, D_HEAD)
                    for ref in (own_ref, other_ref)
                ],
                axis=0,
            )
            for which in range(3)
        )
        parts = []
        for block in blocks:
            grad = jnp.zeros((TILE, D_HEAD), jnp.float32)
            for which in range(3):
                tile = block[first + which * TILE : first + (which + 1) * TILE]
                moved = pltpu.roll(tile, (which * third - rows) % TILE, 0)
                inside = (row >= which * third) & (row < (which + 1) * third)
                grad = jnp.where(inside, moved, grad)
            parts.append(grad)
        grad = jnp.concatenate(parts, axis=0).astype(jnp.bfloat16)
        logits = jnp.where(is_key, dot(key, query, 1, 1), -jnp.inf)
        grad_weights = dot(value, grad, 1, 1)
        top = jnp.max(logits, axis=0, keepdims=True)
        terms = jnp.exp((logits - top) * score_scale)
        inverse = 1.0 / jnp.sum(terms, axis=0, keepdims=True)
        row_dot = jnp.sum(terms * grad_weights, axis=0, keepdims=True) * inverse
        weights = terms * inverse
        grad_low = (weights * (grad_weights - row_dot)).astype(jnp.bfloat16)
        weights_low = weights.astype(jnp.bfloat16)
        grads += [
            dot(grad_low[:, :half], key, 0, 0) * score_scale,
            dot(grad_low[:half], query, 1, 0) * score_scale,
            dot(weights_low[:half], grad, 1, 0),
        ]
    out_ref[...] = jnp.concatenate(
        [
            total[sender * TILE : sender * TILE + rows]
            for sender in places
            for total in grads
        ],
        axis=0,
    ).astype(jnp.bfloat16)


def unpack_kernel(places, in_ref, query_ref, key_ref, value_ref):
    rows = query_ref.shape[0]
    heads = in_ref.shape[0] // (3 * rows)
    received = in_ref[...].astype(jnp.float32)
    for which, ref in enumerate((query_ref, key_ref, value_ref)):
        for place in range(heads):
            first = (3 * place + which) * rows
            head = CORES * places[place // CORES] + place % CORES
            columns = slice(head * D_HEAD, (head + 1) * D_HEAD)
            ref[:, columns] = received[first : first + rows].astype(jnp.bfloat16)


def exchange(chunks, order):
    groups = [
        [CORES * chip + (core ^ (chip in TURNED)) for chip in order] for core in range(CORES)
    ]
    return lax.all_to_all(
        chunks, AXES, split_axis=0, concat_axis=0, tiled=True, axis_index_groups=groups
    )


def by_head(queries, key_vectors, value_vectors, cotangent):
    rows = queries.shape[0]
    if 4 * rows != 3 * TILE:
        return by_block(queries, key_vectors, value_vectors, cotangent)
    chips = HEADS // CORES
    places = [INWARD.index(chip) for chip in OUTWARD]
    packed = pl.pallas_call(
        pack_kernel,
        out_shape=jax.ShapeDtypeStruct((HEADS, 4 * rows, D_HEAD), jnp.bfloat16),
        in_specs=[HBM] * 4,
        out_specs=VMEM,
        scratch_shapes=[
            pltpu.VMEM((4,) + queries.shape, jnp.bfloat16),
            pltpu.SemaphoreType.DMA((2, 4)),
        ],
        compiler_params=PARAMS,
    )(
        *(
            pltpu.with_memory_space_constraint(array, pltpu.HBM)
            for array in (queries, key_vectors, value_vectors, cotangent)
        )
    )
    own = exchange(packed.reshape(chips, CORES * 4 * rows, D_HEAD), INWARD)
    other = lax.ppermute(own, AXES, [(device, device ^ 1) for device in range(HEADS)])
    grads = jax.ShapeDtypeStruct((HEADS * 3 * rows, D_HEAD), jnp.bfloat16)
    back = pl.pallas_call(
        functools.partial(head_kernel, rows, places),
        out_shape=grads,
        in_specs=[VMEM] * 2,
        out_specs=VMEM,
        compiler_params=PARAMS,
    )(own, other)
    back = exchange(back.reshape(chips, CORES * 3 * rows // 2, 2, D_HEAD), OUTWARD)
    out = jax.ShapeDtypeStruct(queries.shape, jnp.bfloat16)
    return pl.pallas_call(
        functools.partial(unpack_kernel, places),
        out_shape=(out,) * 3,
        in_specs=[VMEM],
        out_specs=(VMEM,) * 3,
        compiler_params=PARAMS,
    )(back.reshape(grads.shape))


def scores(query_part, key_part, score_scale):
    return (
        jnp.einsum("qhd,khd->hqk", query_part, key_part, preferred_element_type=jnp.float32)
        * score_scale
    )


def by_block(queries, key_vectors, value_vectors, cotangent):
    ulysses_size = lax.axis_size("ulysses")
    head_dev = HEADS // ulysses_size
    score_scale = 1.0 / math.sqrt(D_HEAD)
    query_heads, key_heads, value_heads, grad_heads = (
        lax.all_to_all(queries, "ulysses", split_axis=1, concat_axis=0, tiled=True),
        lax.all_to_all(key_vectors, "ulysses", split_axis=1, concat_axis=0, tiled=True),
        lax.all_to_all(value_vectors, "ulysses", split_axis=1, concat_axis=0, tiled=True),
        lax.all_to_all(cotangent, "ulysses", split_axis=1, concat_axis=0, tiled=True),
    )
    local_rows = query_heads.shape[0]

    def split_heads(matrix):
        return matrix.reshape(matrix.shape[0], head_dev, D_HEAD)

    own_query = split_heads(query_heads)
    own_key = split_heads(key_heads)
    own_value = split_heads(value_heads)
    own_grad = split_heads(grad_heads)
    held_key, held_value = (
        lax.all_gather(key_heads, "blk", axis=0, tiled=True),
        lax.all_gather(value_heads, "blk", axis=0, tiled=True),
    )
    held_key = split_heads(held_key)
    held_value = split_heads(held_value)
    logits = scores(own_query, held_key, score_scale)
    grad_weights = jnp.einsum(
        "qhd,khd->hqk", own_grad, held_value, preferred_element_type=jnp.float32
    )
    block_top = jnp.max(logits, axis=2)
    exp_terms = jnp.exp(logits - block_top[:, :, None])
    row_total = jnp.sum(exp_terms, axis=2)
    row_sum = jnp.sum(exp_terms * grad_weights, axis=2)
    log_total = block_top + jnp.log(row_total)
    row_dot = row_sum / row_total
    all_log, all_dot = (
        lax.all_gather(log_total.T, "blk", axis=0, tiled=True),
        lax.all_gather(row_dot.T, "blk", axis=0, tiled=True),
    )
    logits = scores(own_query, held_key, score_scale)
    weights = jnp.exp(logits - log_total[:, :, None])
    grad_weights = jnp.einsum(
        "qhd,khd->hqk", own_grad, held_value, preferred_element_type=jnp.float32
    )
    grad_low = (weights * (grad_weights - row_dot[:, :, None])).astype(jnp.bfloat16)
    grad_query = jnp.einsum("hqk,khd->qhd", grad_low, held_key, preferred_element_type=jnp.float32)
    remote_query = split_heads(lax.all_gather(query_heads, "blk", axis=0, tiled=True))
    remote_grad = split_heads(lax.all_gather(grad_heads, "blk", axis=0, tiled=True))
    logits = scores(remote_query, own_key, score_scale)
    weights = jnp.exp(logits - all_log.T[:, :, None])
    grad_weights = jnp.einsum(
        "qhd,khd->hqk", remote_grad, own_value, preferred_element_type=jnp.float32
    )
    grad_low = (weights * (grad_weights - all_dot.T[:, :, None])).astype(jnp.bfloat16)
    weights_low = weights.astype(jnp.bfloat16)
    grad_key = jnp.einsum(
        "hqk,qhd->khd", grad_low, remote_query, preferred_element_type=jnp.float32
    )
    grad_value = jnp.einsum(
        "hqk,qhd->khd", weights_low, remote_grad, preferred_element_type=jnp.float32
    )
    grad_key, grad_value = (grad_key, grad_value)

    def to_rows(summed, factor):
        return (summed * factor).astype(jnp.bfloat16).reshape(local_rows, head_dev * D_HEAD)

    return (
        lax.all_to_all(
            to_rows(grad_query, score_scale), "ulysses", split_axis=0, concat_axis=1, tiled=True
        ),
        lax.all_to_all(
            to_rows(grad_key, score_scale), "ulysses", split_axis=0, concat_axis=1, tiled=True
        ),
        lax.all_to_all(
            to_rows(grad_value, 1.0), "ulysses", split_axis=0, concat_axis=1, tiled=True
        ),
    )


def solution(mesh):
    placed = (
        P(("blk", "ulysses"), None),
        P(("blk", "ulysses"), None),
        P(("blk", "ulysses"), None),
        P(("blk", "ulysses"), None),
    )
    by_heads = mesh.size == HEADS == CORES * len(INWARD) and mesh.shape["ulysses"] % CORES == 0
    local = by_head if by_heads else by_block
    return jax.shard_map(
        local,
        mesh=mesh,
        in_specs=placed,
        out_specs=(
            P(("blk", "ulysses"), None),
            P(("blk", "ulysses"), None),
            P(("blk", "ulysses"), None),
        ),
        check_vma=False,
    )
```
